768 devices in a mesh: pair: 64 (over y, x, core), panel: 12 (over z).
Axes of the slice: x: 4, y: 8, z: 12, core: 2. Of those that a mesh axis runs over, the one named last changes fastest.
Arguments:
- amps: bfloat16 [32768, 6144], P('pair', 'panel'), may hold values from -6 to 6
- pair_energy: float32 [32768], P('pair'), may hold values from -2 to -0.5
- virt_energy: float32 [6144], P('panel'), may hold values from 0.5 to 4
- ladder_rows: int32 [64, 48, 16], P('pair', 'panel'), may hold values from 0 to 47, as said below
- ladder_count: int32 [64, 48], P('pair', 'panel'), may hold values from 1 to 16, as said below
- ladder_tiles: bfloat16 [64, 768, 128, 128], P('pair', 'panel'), may hold values from -0.1875 to 0.1875
- cycle_owner: int32 [49152, 1], P(('pair', 'panel')), may hold values from 0 to 63; in each aligned block of 64 rows (0 to 63, 64 to 127, ...) at most 2 rows name the same one
- cycle_slot: int32 [49152, 1], P(('pair', 'panel')), may hold values from 0 to 15
- cycle_tiles: bfloat16 [64, 192, 128, 128], P('pair', 'panel'), may hold values from -0.5 to 0.5
Outputs:
- residual: float32 [32768, 6144], P('pair', 'panel')
The draws below stay inside these ranges and needn't reach their ends.
Inputs may be any that keep to these rules, and one draw needn't show every extreme that they name: `ladder_rows`: each list names 16 different tiles. Only the first ladder_count entries of a list are live; in every draw some list is full. `cycle_owner`: in the 64 rows of one device no pair index is named more than 2 times, and some index reaches it.
All inputs are finite; a program needn't handle non-finite values.
Results may differ from the reference program's by a relative error of at most 0.00075.
Values may be sent and summed in bfloat16 or wider, within the bound.
A program may use at most 64 MiB of HBM per device.

```python
import math
import jax
import jax.numpy as jnp
import numpy as np
from jax import lax

TB = 128
PR = 512
KP = 4
LMAX = 16
RR = 32
NW = 16
KT = 48
NT = 64
CAP = 2
ROWS = 32768
COLS = 6144
ROUTES = 49152
N_PAIR = 64
N_PANEL = 12


def draw_ladder_rows(key, part):
    key = jax.random.fold_in(key, 11)
    keys = jax.random.split(key, N_PAIR * KT)
    picks = jax.vmap(lambda single: jax.random.permutation(single, KT)[:LMAX])(keys)
    return picks.reshape(N_PAIR, KT, LMAX).astype(jnp.int32)


def draw_ladder_count(key, part):
    key = jax.random.fold_in(key, 12)
    first_key, second_key, third_key = jax.random.split(key, 3)
    first = jax.random.randint(first_key, (N_PAIR, KT), 0, LMAX)
    second = jax.random.randint(second_key, (N_PAIR, KT), 0, LMAX)
    counts = 1 + first * second // LMAX
    chosen = jax.random.randint(third_key, (N_PAIR, 1), 0, KT)
    column = jax.lax.broadcasted_iota(jnp.int32, (N_PAIR, KT), 1)
    return jnp.where(column == chosen, LMAX, counts).astype(jnp.int32)


def plant(entries, rng, least, high):
    spot = [jax.random.randint(jax.random.fold_in(rng, axis), (), 0, length) for axis, length in enumerate(entries.shape)]
    main_axis = entries.shape.index(max(entries.shape))
    next_to = spot[:main_axis] + [(spot[main_axis] + 1) % entries.shape[main_axis]] + spot[main_axis + 1:]
    return entries.at[tuple(spot)].set(least).at[tuple(next_to)].set(high)


def block_scale(own_key, extent, cuts, low, high):
    factor_of = 1.0
    for dim, shards_of in cuts:
        steps = jax.random.uniform(jax.random.fold_in(jax.random.fold_in(own_key, 6), dim), (shards_of,), jnp.float32, low / len(cuts), high / len(cuts))
        factor_of = factor_of * jnp.repeat(jnp.exp(steps), extent[dim] // shards_of).reshape((-1,) + (1,) * (len(extent) - 1 - dim))
    return factor_of


def assign_block(stream_key, own, number, rows, count, top, reach, skew):
    sequence = jax.random.permutation(stream_key, count)
    packed, ordinary = shares(count, rows * top, reach, skew, True), shares(count, rows * top, reach, skew, False)
    places = jnp.arange(count)

    def named(lengths, rotation):
        used = int((lengths > 0).sum())
        fixed = max(1, used // 4)
        moved = fixed + (places - fixed + rotation * (used - fixed)) % max(1, count - fixed)
        return jnp.zeros((count,), jnp.int32).at[sequence[jnp.where(places < fixed, places, moved)]].set(jnp.asarray(lengths, jnp.int32))

    lengths = jnp.where(number % 4 == 0, named(packed, number // 4), named(ordinary, number - number // 4 - 1))
    mixed = jax.random.permutation(jax.random.fold_in(own, 3), count)
    donor, sink = mixed[0:count // 2 * 2:2], mixed[1:count // 2 * 2:2]
    margin = jnp.minimum(lengths[donor] - 1, reach - lengths[sink]) // 2
    margin = jnp.where((donor == sequence[0]) | (sink == sequence[0]) | (lengths[sink] == 0), 0, jnp.maximum(margin, 0))
    moved = jax.random.randint(jax.random.fold_in(own, 4), (count // 2,), 0, 1 << 20) % (margin + 1)
    lengths = lengths.at[donor].add(-moved).at[sink].add(moved)
    members = jnp.searchsorted(jnp.cumsum(lengths), jnp.arange(rows * top), side="right").astype(jnp.int32)
    table = members.reshape(top, rows).T
    table = table[jax.random.permutation(jax.random.fold_in(own, 1), rows)]
    rotation = jax.random.randint(jax.random.fold_in(own, 2), (rows, 1), 0, top)
    return jnp.take_along_axis(table, (jnp.arange(top)[None, :] + rotation) % top, axis=1)


def shares(count, total, reach, lean, full):
    portions = [(1 << 20) // math.isqrt(standing ** lean) + 1 for standing in range(1, count + 1)]
    largest = reach if full else min(reach, max(-(-total // count), total * portions[0] // sum(portions)))
    least = 1 if total - largest >= count - 1 else 0
    holding, spare = [largest] + [least] * (count - 1), total - largest - least * (count - 1)
    while spare > 0:
        movable = [i for i in range(1, count) if holding[i] < largest] or [i for i in range(1, count) if holding[i] < reach]
        mass, remaining = sum([portions[i] for i in movable]), spare
        for i in movable:
            addition = min(reach - holding[i], max(1, remaining * portions[i] // mass), spare)
            holding[i] = holding[i] + addition
            spare = spare - addition
    return np.array(holding)


def bell_draw(stream_key, extent, width, reach, cuts=(), held_as=jnp.bfloat16):
    drawn = width * jax.random.normal(stream_key, extent, jnp.float32)
    if cuts:
        drawn = drawn * block_scale(stream_key, extent, cuts, -0.22, 0.18)
    return jnp.clip(drawn, -reach, reach).astype(held_as)


def setup_inputs(seed: int = 0) -> dict:
    key_of = jax.random.split(jax.random.key(seed), 10)
    amps = bell_draw(key_of[0], (ROWS, COLS), 1.0, 6.0, ((0, 64), (1, 12)))
    pair_energy = jnp.clip(-2.0 + 1.5 * jax.random.uniform(key_of[1], (ROWS,), jnp.float32) ** block_scale(key_of[1], (ROWS,), ((0, 64),), -0.2, 0.2), -2.0, -0.5)
    virt_energy = jnp.clip(0.5 + 3.5 * jax.random.uniform(key_of[2], (COLS,), jnp.float32) ** block_scale(key_of[2], (COLS,), ((0, 12),), -0.2, 0.2), 0.5, 4.0)
    ladder_rows = draw_ladder_rows(jax.random.fold_in(key_of[9], 71), 0)
    ladder_count = draw_ladder_count(jax.random.fold_in(key_of[9], 71), 0)
    ladder_tiles = bell_draw(key_of[5], (N_PAIR, KT * LMAX, TB, TB), (TB * LMAX // 2) ** -0.5, 0.1875, ((0, 64), (1, 12)))
    cycle_owner_keys = jax.random.split(jax.random.fold_in(key_of[6], 1), ROUTES // NT)
    cycle_owner_turns = jax.random.permutation(jax.random.fold_in(key_of[6], 3), ROUTES // NT)
    cycle_owner = jax.vmap(lambda own, number: assign_block(jax.random.fold_in(key_of[6], 2), own, number, NT, N_PAIR, 1, CAP, 2))(cycle_owner_keys, cycle_owner_turns).reshape((ROUTES, 1))
    cycle_slot = plant(jax.random.randint(key_of[7], (ROUTES, 1), 0, NW), jax.random.fold_in(key_of[7], 1), 0, NW - 1).astype(jnp.int32)
    cycle_tiles = bell_draw(key_of[8], (N_PAIR, N_PANEL * NW, TB, TB), TB ** -0.5, 0.5, ((0, 64), (1, 12)))
    return dict(amps=amps, pair_energy=pair_energy, virt_energy=virt_energy, ladder_rows=ladder_rows, ladder_count=ladder_count, ladder_tiles=ladder_tiles, cycle_owner=cycle_owner, cycle_slot=cycle_slot, cycle_tiles=cycle_tiles)


def reference(amps, pair_energy, virt_energy, ladder_rows, ladder_count, ladder_tiles, cycle_owner, cycle_slot, cycle_tiles):
    total_rows, total_cols = amps.shape
    tile_count = total_cols // TB
    slabs = amps.reshape(N_PAIR, PR, tile_count, TB)

    def ladder_slab(inputs):
        block, lists, counts, tiles = inputs
        picked = jnp.take(block, lists.reshape(-1), axis=1).reshape(PR, tile_count, LMAX * TB)
        live_mask = (lax.broadcasted_iota(jnp.int32, (tile_count, LMAX), 1) < counts[:, None]).astype(jnp.bfloat16)
        masked = tiles.reshape(tile_count, LMAX, TB, TB) * live_mask[:, :, None, None]
        return jnp.einsum("rkc,kcd->rkd", picked.astype(jnp.float32), masked.reshape(tile_count, LMAX * TB, TB).astype(jnp.float32))

    ladder = lax.map(ladder_slab, (slabs, ladder_rows, ladder_count, ladder_tiles)).reshape(total_rows, total_cols)

    cycle_input = amps.reshape(N_PAIR, PR // RR, RR, N_PANEL, KP, TB).transpose(0, 3, 1, 4, 2, 5)
    cycle_input = cycle_input.reshape(N_PAIR * N_PANEL, NT, RR, TB)
    owners = cycle_owner.reshape(N_PAIR * N_PANEL, NT)
    slots = cycle_slot.reshape(N_PAIR * N_PANEL, NT)
    panel_of = (jnp.arange(N_PAIR * N_PANEL) % N_PANEL).astype(jnp.int32)
    table = cycle_tiles.reshape(N_PAIR * N_PANEL * NW, TB, TB)

    def cycle_block(inputs):
        tiles, owner_ids, slot_ids, panel_id = inputs
        index = (owner_ids * (N_PANEL * NW) + panel_id * NW + slot_ids).astype(jnp.int32)
        mats = jnp.take(table, index, axis=0)
        return jnp.einsum("trc,tcd->trd", tiles.astype(jnp.float32), mats.astype(jnp.float32)).astype(jnp.bfloat16)

    cycle = lax.map(cycle_block, (cycle_input, owners, slots, panel_of))
    cycle = cycle.reshape(N_PAIR, N_PANEL, PR // RR, KP, RR, TB).transpose(0, 2, 4, 1, 3, 5).reshape(total_rows, total_cols)
    energies = virt_energy[None, :] - pair_energy[:, None]
    return energies * amps.astype(jnp.float32) + ladder + cycle.astype(jnp.float32)
```

```python
import functools

import jax
import jax.numpy as jnp
from jax import lax
from jax.experimental import pallas as pl
from jax.experimental.pallas import tpu as pltpu
from jax.sharding import PartitionSpec as P

TB = 128
LMAX = 16
RR = 32
CAP = 2
KP = 4
MESH = pl.DeviceIdType.MESH

FIRST = 5
GROUP = 8


def kernel(
    n_pair,
    n_panel,
    inv_ref,
    source_ref,
    place_ref,
    amps_ref,
    pair_energy_ref,
    virt_energy_ref,
    slot_ref,
    ladder_hbm,
    cycle_hbm,
    out_ref,
    ladder_ref,
    cycle_ref,
    held,
    own,
    mats,
    send,
    got,
    prod,
    ret,
    got_slot,
    slot_table,
    local_sem,
    right_send,
    right_recv,
    left_send,
    left_recv,
    tile_send,
    tile_recv,
    slot_send,
    slot_recv,
    back_send,
    back_recv,
):
    p = lax.axis_index("pair")
    q = lax.axis_index("panel")
    right = (p, lax.rem(q + 1, n_panel))
    left = (p, lax.rem(q + n_panel - 1, n_panel))
    slab = amps_ref.shape[0]
    row_tiles = slab // RR
    half = n_panel // 2
    steps = KP * (half - 1) + KP // 2

    load_ladder = pltpu.make_async_copy(ladder_hbm, ladder_ref, local_sem.at[0])
    load_cycle = pltpu.make_async_copy(cycle_hbm, cycle_ref, local_sem.at[1])
    load_ladder.start()
    load_cycle.start()

    barrier = pltpu.get_barrier_semaphore()
    for neighbour in (left, right):
        pl.semaphore_signal(barrier, inc=1, device_id=neighbour, device_id_type=MESH)

    def greet(d, carry):
        pl.semaphore_signal(
            barrier, inc=1, device_id=(lax.rem(p + d, n_pair), q), device_id_type=MESH
        )
        return carry

    lax.fori_loop(1, n_pair, greet, 0)
    pl.semaphore_wait(barrier, n_pair + 1)

    def to_right(source, tile, s):
        return pltpu.make_async_remote_copy(
            src_ref=source,
            dst_ref=held.at[tile],
            send_sem=right_send.at[s],
            recv_sem=right_recv.at[s],
            device_id=right,
            device_id_type=MESH,
        )

    def to_left(source, tile, s):
        return pltpu.make_async_remote_copy(
            src_ref=source,
            dst_ref=held.at[tile],
            send_sem=left_send.at[s],
            recv_sem=left_recv.at[s],
            device_id=left,
            device_id_type=MESH,
        )

    for s in range(KP):
        j, k = s, (s + KP // 2) % KP
        to_right(amps_ref.at[:, pl.ds(j * TB, TB)], q * KP + j, s).start()
        to_left(amps_ref.at[:, pl.ds(k * TB, TB)], q * KP + k, s).start()

    for r in range(row_tiles):
        for k in range(KP):
            own[r * KP + k] = amps_ref[pl.ds(r * RR, RR), pl.ds(k * TB, TB)]

    def dispatch(d, carry):
        peer = lax.rem(p + d, n_pair)
        for c in range(CAP):
            send[peer, c] = own[source_ref[0, peer * CAP + c]]
        pltpu.make_async_remote_copy(
            src_ref=send.at[peer],
            dst_ref=got.at[p],
            send_sem=tile_send,
            recv_sem=tile_recv.at[p],
            device_id=(peer, q),
            device_id_type=MESH,
        ).start()
        pltpu.make_async_remote_copy(
            src_ref=slot_ref,
            dst_ref=got_slot.at[p],
            send_sem=slot_send,
            recv_sem=slot_recv,
            device_id=(peer, q),
            device_id_type=MESH,
        ).start()
        return carry

    lax.fori_loop(1, n_pair, dispatch, 0)
    for c in range(CAP):
        got[p, c] = own[source_ref[0, p * CAP + c]]
    got_slot[p] = slot_ref[...]

    for b in range(slab // TB):
        rows = pl.ds(b * TB, TB)
        column = jnp.transpose(
            jnp.broadcast_to(pair_energy_ref[:, rows], (TB, TB)), (1, 0)
        )
        for k in range(KP):
            cols = pl.ds(k * TB, TB)
            out_ref[rows, cols] = (virt_energy_ref[:, cols] - column) * amps_ref[
                rows, cols
            ].astype(jnp.float32)

    load_ladder.wait()
    load_cycle.wait()

    def add_ladder(first, second, first_tile, second_tile):
        for i, tile in enumerate((first_tile, second_tile)):
            for k in range(KP):
                entry = inv_ref[k, tile]
                mat = ladder_ref[k * LMAX + jnp.maximum(entry - 1, 0)]
                mats[pl.ds(i * TB, TB), pl.ds(k * TB, TB)] = jnp.where(
                    entry > 0, mat, jnp.zeros_like(mat)
                )
        lhs = jnp.concatenate([first, second], axis=1)
        for n in range(KP // 2):
            cols = pl.ds(n * 2 * TB, 2 * TB)
            out_ref[:, cols] += jnp.dot(
                lhs, mats[:, cols], preferred_element_type=jnp.float32
            )

    for j in range(0, KP, 2):
        add_ladder(
            amps_ref[:, pl.ds(j * TB, TB)],
            amps_ref[:, pl.ds((j + 1) * TB, TB)],
            q * KP + j,
            q * KP + j + 1,
        )

    def ring(s):
        hop = s // KP + 1
        from_left = lax.rem(q + n_panel - hop, n_panel) * KP + lax.rem(s, KP)
        from_right = lax.rem(q + hop, n_panel) * KP + lax.rem(s + KP // 2, KP)
        to_right(held.at[from_left], from_left, s).wait_recv()

        @pl.when(s < steps - KP)
        def _():
            to_right(held.at[from_left], from_left, s + KP).start()

        to_left(held.at[from_right], from_right, s).wait_recv()

        @pl.when(s < steps - KP)
        def _():
            to_left(held.at[from_right], from_right, s + KP).start()

        add_ladder(held[from_left], held[from_right], from_left, from_right)

    def back(source, s):
        return pltpu.make_async_remote_copy(
            src_ref=prod.at[source],
            dst_ref=ret.at[p],
            send_sem=back_send,
            recv_sem=back_recv,
            device_id=(source, q),
            device_id_type=MESH,
        )

    def multiply(source):
        for c in range(CAP):
            mat = cycle_ref[slot_table[source, 0, p * CAP + c]]
            prod[source, c] = jnp.dot(
                got[source, c], mat, preferred_element_type=jnp.float32
            ).astype(jnp.bfloat16)

    def answer(base, count):
        sources = [lax.rem(p + n_pair - (base + u), n_pair) for u in range(count)]
        for source in sources:
            pltpu.make_async_remote_copy(
                src_ref=send.at[source],
                dst_ref=got.at[source],
                send_sem=tile_send,
                recv_sem=tile_recv.at[source],
                device_id=(source, q),
                device_id_type=MESH,
            ).wait_recv()
        for source in sources:
            multiply(source)
        for source in sources:
            back(source, 0).start()

    others = n_pair - 1
    group = min(GROUP, others)
    chunks = others // group
    rest = others - chunks * group
    first = min(FIRST, max(0, steps - chunks))

    def plain(s, carry):
        ring(s)
        return carry

    def both(s, carry):
        ring(s)
        answer(1 + (s - first) * group, group)
        return carry

    lax.fori_loop(0, first, plain, 0)
    all_slots = pltpu.make_async_remote_copy(
        src_ref=got_slot.at[pl.ds(0, others)],
        dst_ref=got_slot.at[pl.ds(0, others)],
        send_sem=slot_send,
        recv_sem=slot_recv,
        device_id=right,
        device_id_type=MESH,
    )
    all_slots.wait_recv()
    to_table = pltpu.make_async_copy(got_slot, slot_table, local_sem.at[2])
    to_table.start()
    to_table.wait()
    lax.fori_loop(first, first + chunks, both, 0)
    if rest:
        answer(1 + chunks * group, rest)
    multiply(p)
    ret[p] = prod[p]
    lax.fori_loop(first + chunks, steps, plain, 0)

    all_back = pltpu.make_async_remote_copy(
        src_ref=prod.at[pl.ds(0, others)],
        dst_ref=ret.at[pl.ds(0, others)],
        send_sem=back_send,
        recv_sem=back_recv,
        device_id=right,
        device_id_type=MESH,
    )
    all_back.wait_recv()
    for r in range(row_tiles):
        for k in range(KP):
            place = place_ref[0, r * KP + k]
            out_ref[pl.ds(r * RR, RR), pl.ds(k * TB, TB)] += ret[
                place // CAP, lax.rem(place, CAP)
            ].astype(jnp.float32)

    def sent(s, carry):
        to_right(held.at[0], 0, s).wait_send()
        to_left(held.at[0], 0, s).wait_send()
        return carry

    lax.fori_loop(0, steps, sent, 0)
    all_slots.wait_send()
    all_back.wait_send()
    pltpu.make_async_remote_copy(
        src_ref=send.at[pl.ds(0, others)],
        dst_ref=got.at[pl.ds(0, others)],
        send_sem=tile_send,
        recv_sem=back_recv,
        device_id=right,
        device_id_type=MESH,
    ).wait_send()


def on_device(
    n_pair,
    n_panel,
    amps,
    pair_energy,
    virt_energy,
    ladder_rows,
    ladder_count,
    ladder_tiles,
    cycle_owner,
    cycle_slot,
    cycle_tiles,
):
    slab = amps.shape[0]
    tiles = cycle_owner.shape[0]
    steps = KP * (n_panel // 2 - 1) + KP // 2

    lists = ladder_rows[0]
    live = lax.broadcasted_iota(jnp.int32, (KP, LMAX), 1) < ladder_count[0][:, None]
    names = lax.broadcasted_iota(jnp.int32, (KP, LMAX, n_panel * KP), 2)
    order = lax.broadcasted_iota(jnp.int32, (KP, LMAX, n_panel * KP), 1) + 1
    hit = (lists[:, :, None] == names) & live[:, :, None]
    inv = jnp.max(jnp.where(hit, order, 0), axis=1)

    owner = cycle_owner[:, 0]
    code = lax.broadcasted_iota(jnp.int32, (tiles,), 0) * 16 + cycle_slot[:, 0]
    hot = owner[:, None] == lax.broadcasted_iota(jnp.int32, (tiles, n_pair), 1)
    top = tiles * 16 - 1
    low = jnp.min(jnp.where(hot, code[:, None], top), axis=0)
    high = jnp.max(jnp.where(hot, code[:, None], 0), axis=0)
    codes = jnp.stack([low, high], axis=1).reshape(1, n_pair * CAP)
    source = codes // 16
    slots = codes % 16
    same = owner[:, None] == owner[None, :]
    before = lax.broadcasted_iota(jnp.int32, (tiles, tiles), 0) < lax.broadcasted_iota(
        jnp.int32, (tiles, tiles), 1
    )
    second = jnp.any(same & before, axis=0).astype(jnp.int32)
    place = (owner * CAP + second).reshape(1, tiles)

    smem = pl.BlockSpec(memory_space=pltpu.SMEM)
    vmem = pl.BlockSpec(memory_space=pltpu.VMEM)
    anyspace = pl.BlockSpec(memory_space=pl.ANY)
    dma = pltpu.SemaphoreType.DMA
    return pl.pallas_call(
        functools.partial(kernel, n_pair, n_panel),
        out_shape=jax.ShapeDtypeStruct((slab, KP * TB), jnp.float32),
        in_specs=[smem] * 3 + [vmem] * 4 + [anyspace] * 2,
        out_specs=vmem,
        scratch_shapes=[
            pltpu.VMEM((KP * LMAX, TB, TB), jnp.bfloat16),
            pltpu.VMEM((cycle_tiles.shape[1], TB, TB), jnp.bfloat16),
            pltpu.VMEM((n_panel * KP, slab, TB), jnp.bfloat16),
            pltpu.VMEM((tiles, RR, TB), jnp.bfloat16),
            pltpu.VMEM((2 * TB, KP * TB), jnp.bfloat16),
            pltpu.VMEM((n_pair, CAP, RR, TB), jnp.bfloat16),
            pltpu.VMEM((n_pair, CAP, RR, TB), jnp.bfloat16),
            pltpu.VMEM((n_pair, CAP, RR, TB), jnp.bfloat16),
            pltpu.VMEM((n_pair, CAP, RR, TB), jnp.bfloat16),
            pltpu.VMEM((n_pair, 1, n_pair * CAP), jnp.int32),
            pltpu.SMEM((n_pair, 1, n_pair * CAP), jnp.int32),
            dma((3,)),
            dma((steps,)),
            dma((steps,)),
            dma((steps,)),
            dma((steps,)),
            dma(()),
            dma((n_pair,)),
            dma(()),
            dma(()),
            dma(()),
            dma(()),
        ],
        compiler_params=pltpu.CompilerParams(
            collective_id=0, has_side_effects=True, vmem_limit_bytes=40 * 1024 * 1024
        ),
        cost_estimate=pl.CostEstimate(
            flops=4 * 10**9, bytes_accessed=5 * 10**6, transcendentals=0
        ),
    )(
        inv,
        source,
        place,
        amps,
        pair_energy.reshape(1, slab),
        virt_energy.reshape(1, KP * TB),
        slots,
        ladder_tiles[0],
        cycle_tiles[0],
    )


def solution(mesh):
    in_specs = (
        P("pair", "panel"),
        P("pair"),
        P("panel"),
        P("pair", "panel", None),
        P("pair", "panel"),
        P("pair", "panel", None, None),
        P(("pair", "panel"), None),
        P(("pair", "panel"), None),
        P("pair", "panel", None, None),
    )
    return jax.shard_map(
        functools.partial(on_device, mesh.shape["pair"], mesh.shape["panel"]),
        mesh=mesh,
        in_specs=in_specs,
        out_specs=P("pair", "panel"),
        check_vma=False,
    )
```

```python
import functools

import jax
import jax.numpy as jnp
from jax import lax
from jax.experimental import pallas as pl
from jax.experimental.pallas import tpu as pltpu
from jax.sharding import PartitionSpec as P

TB = 128
LMAX = 16
RR = 32
CAP = 2
SLOTS = 16
CODES = 1024
KP = 4
MESH = pl.DeviceIdType.MESH

FIRST = 7
GROUP = 9


def kernel(
    n_pair,
    n_panel,
    owner_hbm,
    slot_hbm,
    lists_hbm,
    count_hbm,
    amps_hbm,
    pair_energy_hbm,
    virt_energy_hbm,
    ladder_hbm,
    cycle_hbm,
    out_hbm,
    owner_ref,
    slot_ref,
    lists_ref,
    count_ref,
    code_row,
    inv_rows,
    code_ref,
    inv_ref,
    amps_ref,
    pair_energy_ref,
    virt_energy_ref,
    out_ref,
    ladder_ref,
    cycle_ref,
    held,
    own,
    mats,
    send,
    got,
    prod,
    ret,
    got_slot,
    slot_table,
    local_sem,
    right_send,
    right_recv,
    left_send,
    left_recv,
    tile_send,
    tile_recv,
    slot_send,
    slot_recv,
    back_send,
    back_recv,
):
    p = lax.axis_index("pair")
    q = lax.axis_index("panel")
    right = (p, lax.rem(q + 1, n_panel))
    left = (p, lax.rem(q + n_panel - 1, n_panel))
    slab = amps_ref.shape[0]
    row_tiles = slab // RR
    half = n_panel // 2
    steps = KP * (half - 1) + KP // 2
    last = steps - 1

    loads = [
        pltpu.make_async_copy(source, target, local_sem.at[i])
        for i, (source, target) in enumerate(
            (
                (amps_hbm, amps_ref),
                (owner_hbm, owner_ref),
                (slot_hbm, slot_ref),
                (lists_hbm, lists_ref),
                (count_hbm, count_ref),
                (pair_energy_hbm, pair_energy_ref),
                (virt_energy_hbm, virt_energy_ref),
                (cycle_hbm, cycle_ref),
                (ladder_hbm, ladder_ref),
            )
        )
    ]
    for load in loads:
        load.start()

    barrier = pltpu.get_barrier_semaphore()
    for neighbour in (left, right):
        pl.semaphore_signal(barrier, inc=1, device_id=neighbour, device_id_type=MESH)

    def greet(d, carry):
        pl.semaphore_signal(
            barrier, inc=1, device_id=(lax.rem(p + d, n_pair), q), device_id_type=MESH
        )
        return carry

    lax.fori_loop(1, n_pair, greet, 0)
    loads[0].wait()
    pl.semaphore_wait(barrier, n_pair + 1)

    def to_right(source, tile, s):
        return pltpu.make_async_remote_copy(
            src_ref=source,
            dst_ref=held.at[tile],
            send_sem=right_send.at[s],
            recv_sem=right_recv.at[s],
            device_id=right,
            device_id_type=MESH,
        )

    def to_left(source, tile, s):
        return pltpu.make_async_remote_copy(
            src_ref=source,
            dst_ref=held.at[tile],
            send_sem=left_send.at[s],
            recv_sem=left_recv.at[s],
            device_id=left,
            device_id_type=MESH,
        )

    for s in range(KP):
        j, k = s, (s + KP // 2) % KP
        to_right(amps_ref.at[:, pl.ds(j * TB, TB)], q * KP + j, s).start()
        to_left(amps_ref.at[:, pl.ds(k * TB, TB)], q * KP + k, s).start()

    for load in loads[1:5]:
        load.wait()
    tiles = row_tiles * KP
    lane = lax.broadcasted_iota(jnp.int32, (1, TB), 1)
    low = jnp.zeros((1, TB), jnp.int32)
    high = jnp.zeros((1, TB), jnp.int32)
    for t in range(tiles):
        u = tiles - 1 - t
        high = jnp.where(lane == owner_ref[0, t], t * SLOTS + slot_ref[0, t], high)
        low = jnp.where(lane == owner_ref[0, u], u * SLOTS + slot_ref[0, u], low)
    code_row[...] = low * CODES + high
    row = lax.broadcasted_iota(jnp.int32, (KP, TB), 0)
    column = lax.broadcasted_iota(jnp.int32, (KP, TB), 1)
    inv = jnp.zeros((KP, TB), jnp.int32)
    for k in range(KP):
        for i in range(LMAX):
            named = jnp.where(i < count_ref[0, k], lists_ref[k, i], -1)
            inv = jnp.where((row == k) & (column == named), i + 1, inv)
    inv_rows[...] = inv
    tables = [
        pltpu.make_async_copy(code_row, code_ref, local_sem.at[9]),
        pltpu.make_async_copy(inv_rows, inv_ref, local_sem.at[10]),
    ]
    for table in tables:
        table.start()

    for r in range(row_tiles):
        for k in range(KP):
            own[r * KP + k] = amps_ref[pl.ds(r * RR, RR), pl.ds(k * TB, TB)]

    for table in tables:
        table.wait()

    def codes_of(code):
        return lax.shift_right_logical(code, 10), lax.bitwise_and(code, CODES - 1)

    def fill(peer, target, place):
        for c, code in enumerate(codes_of(code_ref[0, peer])):
            target[place, c] = own[lax.shift_right_logical(code, 4)]

    def dispatch(d, carry):
        peer = lax.rem(p + d, n_pair)
        fill(peer, send, peer)
        pltpu.make_async_remote_copy(
            src_ref=send.at[peer],
            dst_ref=got.at[p],
            send_sem=tile_send,
            recv_sem=tile_recv.at[p],
            device_id=(peer, q),
            device_id_type=MESH,
        ).start()
        pltpu.make_async_remote_copy(
            src_ref=code_row,
            dst_ref=got_slot.at[p],
            send_sem=slot_send,
            recv_sem=slot_recv,
            device_id=(peer, q),
            device_id_type=MESH,
        ).start()
        return carry

    lax.fori_loop(1, n_pair, dispatch, 0)
    fill(p, got, p)
    got_slot[p] = code_row[...]

    for load in loads[5:]:
        load.wait()
    for b in range(slab // TB):
        rows = pl.ds(b * TB, TB)
        column = jnp.transpose(
            jnp.broadcast_to(pair_energy_ref[:, rows], (TB, TB)), (1, 0)
        )
        for k in range(KP):
            cols = pl.ds(k * TB, TB)
            out_ref[rows, cols] = (virt_energy_ref[:, cols] - column) * amps_ref[
                rows, cols
            ].astype(jnp.float32)

    def pick(first_tile, second_tile):
        for i, tile in enumerate((first_tile, second_tile)):
            for k in range(KP):
                entry = inv_ref[k, tile]
                mat = ladder_ref[k * LMAX + jnp.maximum(entry - 1, 0)]
                mats[pl.ds(i * TB, TB), pl.ds(k * TB, TB)] = jnp.where(
                    entry > 0, mat, jnp.zeros_like(mat)
                )

    def add_ladder(first, second):
        lhs = jnp.concatenate([first, second], axis=1)
        for n in range(KP // 2):
            cols = pl.ds(n * 2 * TB, 2 * TB)
            out_ref[:, cols] += jnp.dot(
                lhs, mats[:, cols], preferred_element_type=jnp.float32
            )

    for j in range(0, KP, 2):
        pick(q * KP + j, q * KP + j + 1)
        add_ladder(
            amps_ref[:, pl.ds(j * TB, TB)], amps_ref[:, pl.ds((j + 1) * TB, TB)]
        )

    def arrivals(s):
        hop = s // KP + 1
        from_left = lax.rem(q + n_panel - hop, n_panel) * KP + lax.rem(s, KP)
        from_right = lax.rem(q + hop, n_panel) * KP + lax.rem(s + KP // 2, KP)
        return from_left, from_right

    def ring(s):
        from_left, from_right = arrivals(s)
        to_right(held.at[from_left], from_left, s).wait_recv()

        @pl.when((s < steps - KP) & ((s < last - KP) | (q != n_panel - 1)))
        def _():
            to_right(held.at[from_left], from_left, s + KP).start()

        to_left(held.at[from_right], from_right, s).wait_recv()

        @pl.when(s < steps - KP)
        def _():
            to_left(held.at[from_right], from_right, s + KP).start()

        @pl.when((s == steps - KP + 1) & (q == 1))
        def _():
            to_left(held.at[from_right], from_right, steps).start()

        pick(from_left, from_right)
        add_ladder(held[from_left], held[from_right])

    def back(source, s):
        return pltpu.make_async_remote_copy(
            src_ref=prod.at[source],
            dst_ref=ret.at[p],
            send_sem=back_send,
            recv_sem=back_recv,
            device_id=(source, q),
            device_id_type=MESH,
        )

    def multiply(source):
        for c, code in enumerate(codes_of(slot_table[source, 0, p])):
            mat = cycle_ref[lax.bitwise_and(code, SLOTS - 1)]
            prod[source, c] = jnp.dot(
                got[source, c], mat, preferred_element_type=jnp.float32
            ).astype(jnp.bfloat16)

    def answer(base, count):
        sources = [lax.rem(p + n_pair - (base + u), n_pair) for u in range(count)]
        for source in sources:
            pltpu.make_async_remote_copy(
                src_ref=send.at[source],
                dst_ref=got.at[source],
                send_sem=tile_send,
                recv_sem=tile_recv.at[source],
                device_id=(source, q),
                device_id_type=MESH,
            ).wait_recv()
        for source in sources:
            multiply(source)
        for source in sources:
            back(source, 0).start()

    others = n_pair - 1
    group = min(GROUP, others)
    chunks = others // group
    rest = others - chunks * group
    first = min(FIRST, max(0, last - chunks))

    def plain(s, carry):
        ring(s)
        return carry

    def both(s, carry):
        ring(s)
        answer(1 + (s - first) * group, group)
        return carry

    lax.fori_loop(0, first, plain, 0)
    all_slots = pltpu.make_async_remote_copy(
        src_ref=got_slot.at[pl.ds(0, others)],
        dst_ref=got_slot.at[pl.ds(0, others)],
        send_sem=slot_send,
        recv_sem=slot_recv,
        device_id=right,
        device_id_type=MESH,
    )
    all_slots.wait_recv()
    to_table = pltpu.make_async_copy(got_slot, slot_table, local_sem.at[11])
    to_table.start()
    to_table.wait()
    lax.fori_loop(first, first + chunks, both, 0)
    if rest:
        answer(1 + chunks * group, rest)
    multiply(p)
    ret[p] = prod[p]
    lax.fori_loop(first + chunks, last, plain, 0)

    all_back = pltpu.make_async_remote_copy(
        src_ref=prod.at[pl.ds(0, others)],
        dst_ref=ret.at[pl.ds(0, others)],
        send_sem=back_send,
        recv_sem=back_recv,
        device_id=right,
        device_id_type=MESH,
    )
    all_back.wait_recv()
    for r in range(row_tiles):
        for k in range(KP):
            t = r * KP + k
            owner = owner_ref[0, t]
            first_code, _ = codes_of(code_ref[0, owner])
            later = (lax.shift_right_logical(first_code, 4) != t).astype(jnp.int32)
            out_ref[pl.ds(r * RR, RR), pl.ds(k * TB, TB)] += ret[owner, later].astype(
                jnp.float32
            )

    from_left, from_right = arrivals(last)
    pick(from_left, from_right)

    def sent(s, carry):
        to_right(held.at[0], 0, s).wait_send()
        to_left(held.at[0], 0, s).wait_send()
        return carry

    lax.fori_loop(0, last, sent, 0)
    to_left(held.at[0], 0, last).wait_send()

    @pl.when(q != n_panel - 1)
    def _():
        to_right(held.at[0], 0, last).wait_send()

    @pl.when(q == 1)
    def _():
        to_left(held.at[0], 0, steps).wait_send()

    all_slots.wait_send()
    all_back.wait_send()
    pltpu.make_async_remote_copy(
        src_ref=send.at[pl.ds(0, others)],
        dst_ref=got.at[pl.ds(0, others)],
        send_sem=tile_send,
        recv_sem=back_recv,
        device_id=right,
        device_id_type=MESH,
    ).wait_send()

    to_left(held.at[from_right], from_right, last).wait_recv()

    @pl.when(q != 0)
    def _():
        to_right(held.at[from_left], from_left, last).wait_recv()

    @pl.when(q == 0)
    def _():
        to_left(held.at[from_left], from_left, steps).wait_recv()

    stores = []
    for b in range(slab // TB):
        rows = pl.ds(b * TB, TB)
        lhs = jnp.concatenate([held[from_left, rows], held[from_right, rows]], axis=1)
        out_ref[rows] += jnp.dot(lhs, mats[...], preferred_element_type=jnp.float32)
        stores.append(
            pltpu.make_async_copy(out_ref.at[rows], out_hbm.at[rows], local_sem.at[b])
        )
        stores[-1].start()
    for store in stores:
        store.wait()


def on_device(
    n_pair,
    n_panel,
    amps,
    pair_energy,
    virt_energy,
    ladder_rows,
    ladder_count,
    ladder_tiles,
    cycle_owner,
    cycle_slot,
    cycle_tiles,
):
    slab = amps.shape[0]
    tiles = cycle_owner.shape[0]
    steps = KP * (n_panel // 2 - 1) + KP // 2

    anyspace = pl.BlockSpec(memory_space=pl.ANY)
    dma = pltpu.SemaphoreType.DMA
    return pl.pallas_call(
        functools.partial(kernel, n_pair, n_panel),
        out_shape=jax.ShapeDtypeStruct((slab, KP * TB), jnp.float32),
        in_specs=[anyspace] * 9,
        out_specs=anyspace,
        scratch_shapes=[
            pltpu.SMEM((1, tiles), jnp.int32),
            pltpu.SMEM((1, tiles), jnp.int32),
            pltpu.SMEM((KP, LMAX), jnp.int32),
            pltpu.SMEM((1, KP), jnp.int32),
            pltpu.VMEM((1, TB), jnp.int32),
            pltpu.VMEM((KP, TB), jnp.int32),
            pltpu.SMEM((1, TB), jnp.int32),
            pltpu.SMEM((KP, TB), jnp.int32),
            pltpu.VMEM((slab, KP * TB), jnp.bfloat16),
            pltpu.VMEM((1, slab), jnp.float32),
            pltpu.VMEM((1, KP * TB), jnp.float32),
            pltpu.VMEM((slab, KP * TB), jnp.float32),
            pltpu.VMEM((KP * LMAX, TB, TB), jnp.bfloat16),
            pltpu.VMEM((cycle_tiles.shape[1], TB, TB), jnp.bfloat16),
            pltpu.VMEM((n_panel * KP, slab, TB), jnp.bfloat16),
            pltpu.VMEM((tiles, RR, TB), jnp.bfloat16),
            pltpu.VMEM((2 * TB, KP * TB), jnp.bfloat16),
            pltpu.VMEM((n_pair, CAP, RR, TB), jnp.bfloat16),
            pltpu.VMEM((n_pair, CAP, RR, TB), jnp.bfloat16),
            pltpu.VMEM((n_pair, CAP, RR, TB), jnp.bfloat16),
            pltpu.VMEM((n_pair, CAP, RR, TB), jnp.bfloat16),
            pltpu.VMEM((n_pair, 1, TB), jnp.int32),
            pltpu.SMEM((n_pair, 1, TB), jnp.int32),
            dma((12,)),
            dma((steps,)),
            dma((steps,)),
            dma((steps + 1,)),
            dma((steps + 1,)),
            dma(()),
            dma((n_pair,)),
            dma(()),
            dma(()),
            dma(()),
            dma(()),
        ],
        compiler_params=pltpu.CompilerParams(
            collective_id=0, has_side_effects=True, vmem_limit_bytes=60 * 1024 * 1024
        ),
        cost_estimate=pl.CostEstimate(
            flops=4 * 10**9, bytes_accessed=5 * 10**6, transcendentals=0
        ),
    )(
        cycle_owner.reshape(1, tiles),
        cycle_slot.reshape(1, tiles),
        ladder_rows[0],
        ladder_count,
        amps,
        pair_energy.reshape(1, slab),
        virt_energy.reshape(1, KP * TB),
        ladder_tiles[0],
        cycle_tiles[0],
    )


def solution(mesh):
    in_specs = (
        P("pair", "panel"),
        P("pair"),
        P("panel"),
        P("pair", "panel", None),
        P("pair", "panel"),
        P("pair", "panel", None, None),
        P(("pair", "panel"), None),
        P(("pair", "panel"), None),
        P("pair", "panel", None, None),
    )
    return jax.shard_map(
        functools.partial(on_device, mesh.shape["pair"], mesh.shape["panel"]),
        mesh=mesh,
        in_specs=in_specs,
        out_specs=P("pair", "panel"),
        check_vma=False,
    )
```

```python
import functools

import jax
import jax.numpy as jnp
from jax import lax
from jax.experimental import pallas as pl
from jax.experimental.pallas import tpu as pltpu
from jax.sharding import PartitionSpec as P

TB = 128
LMAX = 16
RR = 32
CAP = 2
SLOTS = 16
CODES = 1024
KP = 4
WIDE = 4
MESH = pl.DeviceIdType.MESH

FIRST = 7
GROUP = 9


def kernel(
    n_pair,
    n_panel,
    owner_hbm,
    slot_hbm,
    lists_hbm,
    count_hbm,
    amps_hbm,
    pair_energy_hbm,
    virt_energy_hbm,
    ladder_hbm,
    cycle_hbm,
    out_ref,
    owner_ref,
    slot_ref,
    lists_ref,
    count_ref,
    code_row,
    inv_rows,
    code_ref,
    inv_ref,
    amps_ref,
    pair_energy_ref,
    virt_energy_ref,
    ladder_ref,
    cycle_ref,
    held,
    own,
    mats,
    send,
    got,
    prod,
    ret,
    got_slot,
    slot_table,
    local_sem,
    right_send,
    right_recv,
    left_send,
    left_recv,
    tile_send,
    tile_recv,
    slot_send,
    slot_recv,
    back_send,
    back_recv,
    meet,
):
    p = lax.axis_index("pair")
    q = lax.axis_index("panel")
    right = (p, lax.rem(q + 1, n_panel))
    left = (p, lax.rem(q + n_panel - 1, n_panel))
    slab = amps_ref.shape[0]
    row_tiles = slab // RR
    half = n_panel // 2
    steps = KP * (half - 1) + KP // 2
    last = steps - 1

    loads = [
        pltpu.make_async_copy(source, target, local_sem.at[i])
        for i, (source, target) in enumerate(
            (
                (amps_hbm, amps_ref),
                (owner_hbm, owner_ref),
                (slot_hbm, slot_ref),
                (lists_hbm, lists_ref),
                (count_hbm, count_ref),
                (pair_energy_hbm, pair_energy_ref),
                (virt_energy_hbm, virt_energy_ref),
                (cycle_hbm, cycle_ref),
                (ladder_hbm, ladder_ref),
            )
        )
    ]
    for load in loads:
        load.start()

    row = 2 * WIDE
    rows_in_plane = n_pair // row
    core, x, y = lax.rem(p, 2), lax.rem(p // 2, WIDE), p // row

    def device(y, x, core):
        y = lax.rem(y + rows_in_plane, rows_in_plane)
        return ((y * WIDE + lax.rem(x + WIDE, WIDE)) * 2 + core, q)

    across = [device(y, x, 1 - core)]
    along_x = [device(y, x + 1, core), device(y, x - 1, core)]
    along_y = [device(y + 1, x, core), device(y - 1, x, core)]

    barrier = pltpu.get_barrier_semaphore()
    near = [left, right] + across + along_x + along_y
    for neighbour in near:
        pl.semaphore_signal(barrier, inc=1, device_id=neighbour, device_id_type=MESH)
    loads[0].wait()
    pl.semaphore_wait(barrier, len(near))

    def to_right(source, tile, s):
        return pltpu.make_async_remote_copy(
            src_ref=source,
            dst_ref=held.at[tile],
            send_sem=right_send.at[s],
            recv_sem=right_recv.at[s],
            device_id=right,
            device_id_type=MESH,
        )

    def to_left(source, tile, s):
        return pltpu.make_async_remote_copy(
            src_ref=source,
            dst_ref=held.at[tile],
            send_sem=left_send.at[s],
            recv_sem=left_recv.at[s],
            device_id=left,
            device_id_type=MESH,
        )

    for s in range(KP):
        j, k = s, (s + KP // 2) % KP
        to_right(amps_ref.at[:, pl.ds(j * TB, TB)], q * KP + j, s).start()
        to_left(amps_ref.at[:, pl.ds(k * TB, TB)], q * KP + k, s).start()

    def tell(n, group):
        for neighbour in group:
            pl.semaphore_signal(
                meet.at[n], inc=1, device_id=neighbour, device_id_type=MESH
            )

    tell(0, across)
    for load in loads[1:5]:
        load.wait()
    tiles = row_tiles * KP
    lane = lax.broadcasted_iota(jnp.int32, (1, TB), 1)
    low = jnp.zeros((1, TB), jnp.int32)
    high = jnp.zeros((1, TB), jnp.int32)
    for t in range(tiles):
        u = tiles - 1 - t
        high = jnp.where(lane == owner_ref[0, t], t * SLOTS + slot_ref[0, t], high)
        low = jnp.where(lane == owner_ref[0, u], u * SLOTS + slot_ref[0, u], low)
    code_row[...] = low * CODES + high
    output = lax.broadcasted_iota(jnp.int32, (KP, TB), 0)
    column = lax.broadcasted_iota(jnp.int32, (KP, TB), 1)
    inv = jnp.zeros((KP, TB), jnp.int32)
    for k in range(KP):
        for i in range(LMAX):
            named = jnp.where(i < count_ref[0, k], lists_ref[k, i], -1)
            inv = jnp.where((output == k) & (column == named), i + 1, inv)
    inv_rows[...] = inv
    tables = [
        pltpu.make_async_copy(code_row, code_ref, local_sem.at[9]),
        pltpu.make_async_copy(inv_rows, inv_ref, local_sem.at[10]),
    ]
    for table in tables:
        table.start()
    pl.semaphore_wait(meet.at[0], 1)
    tell(1, along_x)

    for r in range(row_tiles):
        for k in range(KP):
            own[r * KP + k] = amps_ref[pl.ds(r * RR, RR), pl.ds(k * TB, TB)]

    for table in tables:
        table.wait()

    def codes_of(code):
        return lax.shift_right_logical(code, 10), lax.bitwise_and(code, CODES - 1)

    def fill(peer, target, place):
        for c, code in enumerate(codes_of(code_ref[0, peer])):
            target[place, c] = own[lax.shift_right_logical(code, 4)]

    def steps_of(i):
        h = (i // row + 1) // 2
        return lax.select(lax.rem(i // row, 2) == 1, h, rows_in_plane - h), lax.rem(i, row)

    def at(down, over):
        return lax.rem(y + down, rows_in_plane) * row + lax.rem(p + over, row)

    def dispatch(i, carry):
        down, over = steps_of(i)
        peer = at(down, over)
        fill(peer, send, peer)
        pltpu.make_async_remote_copy(
            src_ref=send.at[peer],
            dst_ref=got.at[p],
            send_sem=tile_send,
            recv_sem=tile_recv.at[p],
            device_id=(peer, q),
            device_id_type=MESH,
        ).start()
        pltpu.make_async_remote_copy(
            src_ref=code_row,
            dst_ref=got_slot.at[p],
            send_sem=slot_send,
            recv_sem=slot_recv,
            device_id=(peer, q),
            device_id_type=MESH,
        ).start()
        return carry

    pl.semaphore_wait(meet.at[1], 2)
    lax.fori_loop(1, row, dispatch, 0)
    for r in range(1, rows_in_plane // 2 + 1):
        tell(1 + r, along_y)
        pl.semaphore_wait(meet.at[1 + r], 2)
        begin = (2 * r - 1) * row
        lax.fori_loop(begin, min(begin + 2 * row, n_pair), dispatch, 0)
    fill(p, got, p)
    got_slot[p] = code_row[...]

    for load in loads[5:]:
        load.wait()
    for b in range(slab // TB):
        rows = pl.ds(b * TB, TB)
        column = jnp.transpose(
            jnp.broadcast_to(pair_energy_ref[:, rows], (TB, TB)), (1, 0)
        )
        for k in range(KP):
            cols = pl.ds(k * TB, TB)
            out_ref[rows, cols] = (virt_energy_ref[:, cols] - column) * amps_ref[
                rows, cols
            ].astype(jnp.float32)

    def pick(first_tile, second_tile):
        for i, tile in enumerate((first_tile, second_tile)):
            for k in range(KP):
                entry = inv_ref[k, tile]
                mat = ladder_ref[k * LMAX + jnp.maximum(entry - 1, 0)]
                mats[pl.ds(i * TB, TB), pl.ds(k * TB, TB)] = jnp.where(
                    entry > 0, mat, jnp.zeros_like(mat)
                )

    def add_ladder(first, second):
        lhs = jnp.concatenate([first, second], axis=1)
        for n in range(KP // 2):
            cols = pl.ds(n * 2 * TB, 2 * TB)
            out_ref[:, cols] += jnp.dot(
                lhs, mats[:, cols], preferred_element_type=jnp.float32
            )

    for j in range(0, KP, 2):
        pick(q * KP + j, q * KP + j + 1)
        add_ladder(
            amps_ref[:, pl.ds(j * TB, TB)], amps_ref[:, pl.ds((j + 1) * TB, TB)]
        )

    def arrivals(s):
        hop = s // KP + 1
        from_left = lax.rem(q + n_panel - hop, n_panel) * KP + lax.rem(s, KP)
        from_right = lax.rem(q + hop, n_panel) * KP + lax.rem(s + KP // 2, KP)
        return from_left, from_right

    def ring(s):
        from_left, from_right = arrivals(s)
        to_right(held.at[from_left], from_left, s).wait_recv()

        @pl.when((s < steps - KP) & ((s < last - KP) | (q != n_panel - 1)))
        def _():
            to_right(held.at[from_left], from_left, s + KP).start()

        to_left(held.at[from_right], from_right, s).wait_recv()

        @pl.when(s < steps - KP)
        def _():
            to_left(held.at[from_right], from_right, s + KP).start()

        @pl.when((s == steps - KP + 1) & (q == 1))
        def _():
            to_left(held.at[from_right], from_right, steps).start()

        pick(from_left, from_right)
        add_ladder(held[from_left], held[from_right])

    def back(source, s):
        return pltpu.make_async_remote_copy(
            src_ref=prod.at[source],
            dst_ref=ret.at[p],
            send_sem=back_send,
            recv_sem=back_recv,
            device_id=(source, q),
            device_id_type=MESH,
        )

    def multiply(source):
        for c, code in enumerate(codes_of(slot_table[source, 0, p])):
            mat = cycle_ref[lax.bitwise_and(code, SLOTS - 1)]
            prod[source, c] = jnp.dot(
                got[source, c], mat, preferred_element_type=jnp.float32
            ).astype(jnp.bfloat16)

    def answer(base, count):
        sources = []
        for u in range(count):
            down, over = steps_of(base + u)
            sources.append(at(rows_in_plane - down, row - over))
        for source in sources:
            pltpu.make_async_remote_copy(
                src_ref=send.at[source],
                dst_ref=got.at[source],
                send_sem=tile_send,
                recv_sem=tile_recv.at[source],
                device_id=(source, q),
                device_id_type=MESH,
            ).wait_recv()
        for source in sources:
            multiply(source)
        for source in sources:
            back(source, 0).start()

    others = n_pair - 1
    group = min(GROUP, others)
    chunks = others // group
    rest = others - chunks * group
    first = min(FIRST, max(0, last - chunks))

    def plain(s, carry):
        ring(s)
        return carry

    def both(s, carry):
        ring(s)
        answer(1 + (s - first) * group, group)
        return carry

    lax.fori_loop(0, first, plain, 0)
    all_slots = pltpu.make_async_remote_copy(
        src_ref=got_slot.at[pl.ds(0, others)],
        dst_ref=got_slot.at[pl.ds(0, others)],
        send_sem=slot_send,
        recv_sem=slot_recv,
        device_id=right,
        device_id_type=MESH,
    )
    all_slots.wait_recv()
    to_table = pltpu.make_async_copy(got_slot, slot_table, local_sem.at[11])
    to_table.start()
    to_table.wait()
    lax.fori_loop(first, first + chunks, both, 0)
    if rest:
        answer(1 + chunks * group, rest)
    multiply(p)
    ret[p] = prod[p]
    lax.fori_loop(first + chunks, last, plain, 0)

    all_back = pltpu.make_async_remote_copy(
        src_ref=prod.at[pl.ds(0, others)],
        dst_ref=ret.at[pl.ds(0, others)],
        send_sem=back_send,
        recv_sem=back_recv,
        device_id=right,
        device_id_type=MESH,
    )
    all_back.wait_recv()
    for r in range(row_tiles):
        for k in range(KP):
            t = r * KP + k
            owner = owner_ref[0, t]
            first_code, _ = codes_of(code_ref[0, owner])
            later = (lax.shift_right_logical(first_code, 4) != t).astype(jnp.int32)
            out_ref[pl.ds(r * RR, RR), pl.ds(k * TB, TB)] += ret[owner, later].astype(
                jnp.float32
            )

    from_left, from_right = arrivals(last)
    pick(from_left, from_right)

    def sent(s, carry):
        to_right(held.at[0], 0, s).wait_send()
        to_left(held.at[0], 0, s).wait_send()
        return carry

    lax.fori_loop(0, last, sent, 0)
    to_left(held.at[0], 0, last).wait_send()

    @pl.when(q != n_panel - 1)
    def _():
        to_right(held.at[0], 0, last).wait_send()

    @pl.when(q == 1)
    def _():
        to_left(held.at[0], 0, steps).wait_send()

    all_slots.wait_send()
    all_back.wait_send()
    pltpu.make_async_remote_copy(
        src_ref=send.at[pl.ds(0, others)],
        dst_ref=got.at[pl.ds(0, others)],
        send_sem=tile_send,
        recv_sem=back_recv,
        device_id=right,
        device_id_type=MESH,
    ).wait_send()

    to_left(held.at[from_right], from_right, last).wait_recv()

    @pl.when(q != 0)
    def _():
        to_right(held.at[from_left], from_left, last).wait_recv()

    @pl.when(q == 0)
    def _():
        to_left(held.at[from_left], from_left, steps).wait_recv()

    for b in range(slab // TB):
        rows = pl.ds(b * TB, TB)
        lhs = jnp.concatenate([held[from_left, rows], held[from_right, rows]], axis=1)
        out_ref[rows] += jnp.dot(lhs, mats[...], preferred_element_type=jnp.float32)


def on_device(
    n_pair,
    n_panel,
    amps,
    pair_energy,
    virt_energy,
    ladder_rows,
    ladder_count,
    ladder_tiles,
    cycle_owner,
    cycle_slot,
    cycle_tiles,
):
    slab = amps.shape[0]
    tiles = cycle_owner.shape[0]
    steps = KP * (n_panel // 2 - 1) + KP // 2

    anyspace = pl.BlockSpec(memory_space=pl.ANY)
    dma = pltpu.SemaphoreType.DMA
    return pl.pallas_call(
        functools.partial(kernel, n_pair, n_panel),
        out_shape=pltpu.VMEM((slab, KP * TB), jnp.float32),
        in_specs=[anyspace] * 9,
        out_specs=pl.BlockSpec(memory_space=pltpu.VMEM),
        scratch_shapes=[
            pltpu.SMEM((1, tiles), jnp.int32),
            pltpu.SMEM((1, tiles), jnp.int32),
            pltpu.SMEM((KP, LMAX), jnp.int32),
            pltpu.SMEM((1, KP), jnp.int32),
            pltpu.VMEM((1, TB), jnp.int32),
            pltpu.VMEM((KP, TB), jnp.int32),
            pltpu.SMEM((1, TB), jnp.int32),
            pltpu.SMEM((KP, TB), jnp.int32),
            pltpu.VMEM((slab, KP * TB), jnp.bfloat16),
            pltpu.VMEM((1, slab), jnp.float32),
            pltpu.VMEM((1, KP * TB), jnp.float32),
            pltpu.VMEM((KP * LMAX, TB, TB), jnp.bfloat16),
            pltpu.VMEM((cycle_tiles.shape[1], TB, TB), jnp.bfloat16),
            pltpu.VMEM((n_panel * KP, slab, TB), jnp.bfloat16),
            pltpu.VMEM((tiles, RR, TB), jnp.bfloat16),
            pltpu.VMEM((2 * TB, KP * TB), jnp.bfloat16),
            pltpu.VMEM((n_pair, CAP, RR, TB), jnp.bfloat16),
            pltpu.VMEM((n_pair, CAP, RR, TB), jnp.bfloat16),
            pltpu.VMEM((n_pair, CAP, RR, TB), jnp.bfloat16),
            pltpu.VMEM((n_pair, CAP, RR, TB), jnp.bfloat16),
            pltpu.VMEM((n_pair, 1, TB), jnp.int32),
            pltpu.SMEM((n_pair, 1, TB), jnp.int32),
            dma((12,)),
            dma((steps,)),
            dma((steps,)),
            dma((steps + 1,)),
            dma((steps + 1,)),
            dma(()),
            dma((n_pair,)),
            dma(()),
            dma(()),
            dma(()),
            dma(()),
            pltpu.SemaphoreType.REGULAR((2 + n_pair // (4 * WIDE),)),
        ],
        compiler_params=pltpu.CompilerParams(
            collective_id=0, has_side_effects=True, vmem_limit_bytes=60 * 1024 * 1024
        ),
        cost_estimate=pl.CostEstimate(
            flops=4 * 10**9, bytes_accessed=5 * 10**6, transcendentals=0
        ),
    )(
        cycle_owner.reshape(1, tiles),
        cycle_slot.reshape(1, tiles),
        ladder_rows[0],
        ladder_count,
        amps,
        pair_energy.reshape(1, slab),
        virt_energy.reshape(1, KP * TB),
        ladder_tiles[0],
        cycle_tiles[0],
    )


def solution(mesh):
    in_specs = (
        P("pair", "panel"),
        P("pair"),
        P("panel"),
        P("pair", "panel", None),
        P("pair", "panel"),
        P("pair", "panel", None, None),
        P(("pair", "panel"), None),
        P(("pair", "panel"), None),
        P("pair", "panel", None, None),
    )
    return jax.shard_map(
        functools.partial(on_device, mesh.shape["pair"], mesh.shape["panel"]),
        mesh=mesh,
        in_specs=in_specs,
        out_specs=P("pair", "panel"),
        check_vma=False,
    )
```

```python
import functools

import jax
import jax.numpy as jnp
from jax import lax
from jax.experimental import pallas as pl
from jax.experimental.pallas import tpu as pltpu
from jax.sharding import PartitionSpec as P

TB = 128
LMAX = 16
RR = 32
CAP = 2
SLOTS = 16
CODES = 1024
KP = 4
WIDE = 4
MESH = pl.DeviceIdType.MESH

FIRST = 8
GROUP = 11


def kernel(
    n_pair,
    n_panel,
    owner_hbm,
    slot_hbm,
    lists_hbm,
    count_hbm,
    amps_hbm,
    pair_energy_hbm,
    virt_energy_hbm,
    ladder_hbm,
    cycle_hbm,
    out_ref,
    owner_ref,
    slot_ref,
    lists_ref,
    count_ref,
    code_row,
    inv_rows,
    code_ref,
    inv_ref,
    amps_ref,
    pair_energy_ref,
    virt_energy_ref,
    ladder_ref,
    cycle_ref,
    held,
    own,
    mats,
    send,
    got,
    prod,
    ret,
    got_slot,
    slot_table,
    local_sem,
    right_send,
    right_recv,
    left_send,
    left_recv,
    tile_send,
    tile_recv,
    slot_send,
    slot_recv,
    back_send,
    back_recv,
    meet,
):
    p = lax.axis_index("pair")
    q = lax.axis_index("panel")
    right = (p, lax.rem(q + 1, n_panel))
    left = (p, lax.rem(q + n_panel - 1, n_panel))
    slab = amps_ref.shape[0]
    row_tiles = slab // RR
    half = n_panel // 2
    steps = KP * (half - 1) + KP // 2
    last = steps - 1

    loads = [
        pltpu.make_async_copy(source, target, local_sem.at[i])
        for i, (source, target) in enumerate(
            (
                (amps_hbm, amps_ref),
                (owner_hbm, owner_ref),
                (slot_hbm, slot_ref),
                (lists_hbm, lists_ref),
                (count_hbm, count_ref),
                (pair_energy_hbm, pair_energy_ref),
                (virt_energy_hbm, virt_energy_ref),
                (cycle_hbm, cycle_ref),
                (ladder_hbm, ladder_ref),
            )
        )
    ]
    for load in loads:
        load.start()

    row = 2 * WIDE
    rows_in_plane = n_pair // row
    core, x, y = lax.rem(p, 2), lax.rem(p // 2, WIDE), p // row

    def device(y, x, core):
        y = lax.rem(y + rows_in_plane, rows_in_plane)
        return ((y * WIDE + lax.rem(x + WIDE, WIDE)) * 2 + core, q)

    across = [device(y, x, 1 - core)]
    along_x = [device(y, x + 1, core), device(y, x - 1, core)]
    along_y = [device(y + 1, x, core), device(y - 1, x, core)]
    further_y = [device(y + 2, x, core), device(y - 2, x, core)]

    barrier = pltpu.get_barrier_semaphore()
    near = [left, right] + across + along_x + along_y
    for neighbour in near:
        pl.semaphore_signal(barrier, inc=1, device_id=neighbour, device_id_type=MESH)
    loads[0].wait()
    pl.semaphore_wait(barrier, len(near))

    def to_right(source, tile, s):
        return pltpu.make_async_remote_copy(
            src_ref=source,
            dst_ref=held.at[tile],
            send_sem=right_send.at[s],
            recv_sem=right_recv.at[s],
            device_id=right,
            device_id_type=MESH,
        )

    def to_left(source, tile, s):
        return pltpu.make_async_remote_copy(
            src_ref=source,
            dst_ref=held.at[tile],
            send_sem=left_send.at[s],
            recv_sem=left_recv.at[s],
            device_id=left,
            device_id_type=MESH,
        )

    for s in range(KP):
        j, k = s, (s + KP // 2) % KP
        to_right(amps_ref.at[:, pl.ds(j * TB, TB)], q * KP + j, s).start()
        to_left(amps_ref.at[:, pl.ds(k * TB, TB)], q * KP + k, s).start()

    def arrivals(s):
        hop = s // KP + 1
        from_left = lax.rem(q + n_panel - hop, n_panel) * KP + lax.rem(s, KP)
        from_right = lax.rem(q + hop, n_panel) * KP + lax.rem(s + KP // 2, KP)
        return from_left, from_right

    def forward(s):
        from_left, from_right = arrivals(s)
        to_right(held.at[from_left], from_left, s).wait_recv()

        @pl.when((s < steps - KP) & ((s < last - KP) | (q != n_panel - 1)))
        def _():
            to_right(held.at[from_left], from_left, s + KP).start()

        to_left(held.at[from_right], from_right, s).wait_recv()

        @pl.when(s < steps - KP)
        def _():
            to_left(held.at[from_right], from_right, s + KP).start()

        @pl.when((s == steps - KP + 1) & (q == 1))
        def _():
            to_left(held.at[from_right], from_right, steps).start()

    def tell(n, group):
        for neighbour in group:
            pl.semaphore_signal(
                meet.at[n], inc=1, device_id=neighbour, device_id_type=MESH
            )

    tell(0, across)
    for load in loads[1:5]:
        load.wait()
    tiles = row_tiles * KP
    lane = lax.broadcasted_iota(jnp.int32, (1, TB), 1)
    low = jnp.zeros((1, TB), jnp.int32)
    high = jnp.zeros((1, TB), jnp.int32)
    for t in range(tiles):
        u = tiles - 1 - t
        high = jnp.where(lane == owner_ref[0, t], t * SLOTS + slot_ref[0, t], high)
        low = jnp.where(lane == owner_ref[0, u], u * SLOTS + slot_ref[0, u], low)
    code_row[...] = low * CODES + high
    code_table = pltpu.make_async_copy(code_row, code_ref, local_sem.at[9])
    code_table.start()
    pl.semaphore_wait(meet.at[0], 1)
    tell(1, along_x)

    for r in range(row_tiles):
        for k in range(KP):
            own[r * KP + k] = amps_ref[pl.ds(r * RR, RR), pl.ds(k * TB, TB)]

    pl.semaphore_wait(meet.at[1], 2)
    tell(2, along_y)
    code_table.wait()

    def codes_of(code):
        return lax.shift_right_logical(code, 10), lax.bitwise_and(code, CODES - 1)

    def fill(peer, target, place):
        for c, code in enumerate(codes_of(code_ref[0, peer])):
            target[place, c] = own[lax.shift_right_logical(code, 4)]

    def steps_of(i):
        h = (i // row + 1) // 2
        return lax.select(lax.rem(i // row, 2) == 1, h, rows_in_plane - h), lax.rem(i, row)

    def at(down, over):
        return lax.rem(y + down, rows_in_plane) * row + lax.rem(p + over, row)

    def dispatch(i, carry):
        down, over = steps_of(i)
        peer = at(down, over)
        fill(peer, send, peer)
        pltpu.make_async_remote_copy(
            src_ref=send.at[peer],
            dst_ref=got.at[p],
            send_sem=tile_send,
            recv_sem=tile_recv.at[p],
            device_id=(peer, q),
            device_id_type=MESH,
        ).start()
        pltpu.make_async_remote_copy(
            src_ref=code_row,
            dst_ref=got_slot.at[p],
            send_sem=slot_send,
            recv_sem=slot_recv,
            device_id=(peer, q),
            device_id_type=MESH,
        ).start()
        return carry

    lax.fori_loop(1, row, dispatch, 0)
    rounds = [along_y] if rows_in_plane == 2 else [along_y, further_y, along_y]
    known = [0, 1] if rows_in_plane == 2 else [0, 1, 3, 4]
    for r in range(len(rounds)):
        pl.semaphore_wait(meet.at[2 + r], 2)
        if r + 1 < len(rounds):
            tell(3 + r, rounds[r + 1])
        begin = (2 * known[r] + 1) * row
        end = min((2 * known[r + 1] + 1) * row, n_pair)
        lax.fori_loop(begin, end, dispatch, 0)

    output = lax.broadcasted_iota(jnp.int32, (KP, TB), 0)
    column = lax.broadcasted_iota(jnp.int32, (KP, TB), 1)
    inv = jnp.zeros((KP, TB), jnp.int32)
    for k in range(KP):
        for i in range(LMAX):
            named = jnp.where(i < count_ref[0, k], lists_ref[k, i], -1)
            inv = jnp.where((output == k) & (column == named), i + 1, inv)
    inv_rows[...] = inv
    inv_table = pltpu.make_async_copy(inv_rows, inv_ref, local_sem.at[10])
    inv_table.start()
    fill(p, got, p)
    got_slot[p] = code_row[...]

    for load in loads[5:]:
        load.wait()
    inv_table.wait()
    for b in range(slab // TB):
        rows = pl.ds(b * TB, TB)
        column = jnp.transpose(
            jnp.broadcast_to(pair_energy_ref[:, rows], (TB, TB)), (1, 0)
        )
        for k in range(KP):
            cols = pl.ds(k * TB, TB)
            out_ref[rows, cols] = (virt_energy_ref[:, cols] - column) * amps_ref[
                rows, cols
            ].astype(jnp.float32)

    def pick(first_tile, second_tile):
        for i, tile in enumerate((first_tile, second_tile)):
            for k in range(KP):
                entry = inv_ref[k, tile]
                mat = ladder_ref[k * LMAX + jnp.maximum(entry - 1, 0)]
                mats[pl.ds(i * TB, TB), pl.ds(k * TB, TB)] = jnp.where(
                    entry > 0, mat, jnp.zeros_like(mat)
                )

    def add_ladder(first, second):
        lhs = jnp.concatenate([first, second], axis=1)
        for n in range(KP // 2):
            cols = pl.ds(n * 2 * TB, 2 * TB)
            out_ref[:, cols] += jnp.dot(
                lhs, mats[:, cols], preferred_element_type=jnp.float32
            )

    for j in range(0, KP, 2):
        pick(q * KP + j, q * KP + j + 1)
        add_ladder(
            amps_ref[:, pl.ds(j * TB, TB)], amps_ref[:, pl.ds((j + 1) * TB, TB)]
        )

    def accumulate(s, carry):
        from_left, from_right = arrivals(s)
        pick(from_left, from_right)
        add_ladder(held[from_left], held[from_right])
        return carry

    def back(source, s):
        return pltpu.make_async_remote_copy(
            src_ref=prod.at[source],
            dst_ref=ret.at[p],
            send_sem=back_send,
            recv_sem=back_recv,
            device_id=(source, q),
            device_id_type=MESH,
        )

    def multiply(source):
        for c, code in enumerate(codes_of(slot_table[source, 0, p])):
            mat = cycle_ref[lax.bitwise_and(code, SLOTS - 1)]
            prod[source, c] = jnp.dot(
                got[source, c], mat, preferred_element_type=jnp.float32
            ).astype(jnp.bfloat16)

    def answer(base, count):
        sources = []
        for u in range(count):
            down, over = steps_of(base + u)
            sources.append(at(rows_in_plane - down, row - over))
        for source in sources:
            pltpu.make_async_remote_copy(
                src_ref=send.at[source],
                dst_ref=got.at[source],
                send_sem=tile_send,
                recv_sem=tile_recv.at[source],
                device_id=(source, q),
                device_id_type=MESH,
            ).wait_recv()
        for source in sources:
            multiply(source)
        for source in sources:
            back(source, 0).start()

    others = n_pair - 1
    group = min(GROUP, others)
    chunks = others // group
    rest = others - chunks * group
    first = min(FIRST, max(0, last - chunks))

    def plain(s, carry):
        forward(s)
        return accumulate(s, carry)

    def both(s, carry):
        forward(s)
        accumulate(s, carry)
        answer(1 + (s - first) * group, group)
        return carry

    lax.fori_loop(0, first, plain, 0)
    all_slots = pltpu.make_async_remote_copy(
        src_ref=got_slot.at[pl.ds(0, others)],
        dst_ref=got_slot.at[pl.ds(0, others)],
        send_sem=slot_send,
        recv_sem=slot_recv,
        device_id=right,
        device_id_type=MESH,
    )
    all_slots.wait_recv()
    to_table = pltpu.make_async_copy(got_slot, slot_table, local_sem.at[11])
    to_table.start()
    to_table.wait()
    lax.fori_loop(first, first + chunks, both, 0)
    if rest:
        answer(1 + chunks * group, rest)
    multiply(p)
    ret[p] = prod[p]
    lax.fori_loop(first + chunks, last, plain, 0)

    all_back = pltpu.make_async_remote_copy(
        src_ref=prod.at[pl.ds(0, others)],
        dst_ref=ret.at[pl.ds(0, others)],
        send_sem=back_send,
        recv_sem=back_recv,
        device_id=right,
        device_id_type=MESH,
    )
    all_back.wait_recv()
    for r in range(row_tiles):
        for k in range(KP):
            t = r * KP + k
            owner = owner_ref[0, t]
            first_code, _ = codes_of(code_ref[0, owner])
            later = (lax.shift_right_logical(first_code, 4) != t).astype(jnp.int32)
            out_ref[pl.ds(r * RR, RR), pl.ds(k * TB, TB)] += ret[owner, later].astype(
                jnp.float32
            )

    from_left, from_right = arrivals(last)
    pick(from_left, from_right)

    def sent(s, carry):
        to_right(held.at[0], 0, s).wait_send()
        to_left(held.at[0], 0, s).wait_send()
        return carry

    lax.fori_loop(0, last, sent, 0)
    to_left(held.at[0], 0, last).wait_send()

    @pl.when(q != n_panel - 1)
    def _():
        to_right(held.at[0], 0, last).wait_send()

    @pl.when(q == 1)
    def _():
        to_left(held.at[0], 0, steps).wait_send()

    all_slots.wait_send()
    all_back.wait_send()
    pltpu.make_async_remote_copy(
        src_ref=send.at[pl.ds(0, others)],
        dst_ref=got.at[pl.ds(0, others)],
        send_sem=tile_send,
        recv_sem=back_recv,
        device_id=right,
        device_id_type=MESH,
    ).wait_send()

    to_left(held.at[from_right], from_right, last).wait_recv()

    @pl.when(q != 0)
    def _():
        to_right(held.at[from_left], from_left, last).wait_recv()

    @pl.when(q == 0)
    def _():
        to_left(held.at[from_left], from_left, steps).wait_recv()

    for b in range(slab // TB):
        rows = pl.ds(b * TB, TB)
        lhs = jnp.concatenate([held[from_left, rows], held[from_right, rows]], axis=1)
        out_ref[rows] += jnp.dot(lhs, mats[...], preferred_element_type=jnp.float32)


def on_device(
    n_pair,
    n_panel,
    amps,
    pair_energy,
    virt_energy,
    ladder_rows,
    ladder_count,
    ladder_tiles,
    cycle_owner,
    cycle_slot,
    cycle_tiles,
):
    slab = amps.shape[0]
    tiles = cycle_owner.shape[0]
    steps = KP * (n_panel // 2 - 1) + KP // 2

    anyspace = pl.BlockSpec(memory_space=pl.ANY)
    dma = pltpu.SemaphoreType.DMA
    return pl.pallas_call(
        functools.partial(kernel, n_pair, n_panel),
        out_shape=pltpu.VMEM((slab, KP * TB), jnp.float32),
        in_specs=[anyspace] * 9,
        out_specs=pl.BlockSpec(memory_space=pltpu.VMEM),
        scratch_shapes=[
            pltpu.SMEM((1, tiles), jnp.int32),
            pltpu.SMEM((1, tiles), jnp.int32),
            pltpu.SMEM((KP, LMAX), jnp.int32),
            pltpu.SMEM((1, KP), jnp.int32),
            pltpu.VMEM((1, TB), jnp.int32),
            pltpu.VMEM((KP, TB), jnp.int32),
            pltpu.SMEM((1, TB), jnp.int32),
            pltpu.SMEM((KP, TB), jnp.int32),
            pltpu.VMEM((slab, KP * TB), jnp.bfloat16),
            pltpu.VMEM((1, slab), jnp.float32),
            pltpu.VMEM((1, KP * TB), jnp.float32),
            pltpu.VMEM((KP * LMAX, TB, TB), jnp.bfloat16),
            pltpu.VMEM((cycle_tiles.shape[1], TB, TB), jnp.bfloat16),
            pltpu.VMEM((n_panel * KP, slab, TB), jnp.bfloat16),
            pltpu.VMEM((tiles, RR, TB), jnp.bfloat16),
            pltpu.VMEM((2 * TB, KP * TB), jnp.bfloat16),
            pltpu.VMEM((n_pair, CAP, RR, TB), jnp.bfloat16),
            pltpu.VMEM((n_pair, CAP, RR, TB), jnp.bfloat16),
            pltpu.VMEM((n_pair, CAP, RR, TB), jnp.bfloat16),
            pltpu.VMEM((n_pair, CAP, RR, TB), jnp.bfloat16),
            pltpu.VMEM((n_pair, 1, TB), jnp.int32),
            pltpu.SMEM((n_pair, 1, TB), jnp.int32),
            dma((12,)),
            dma((steps,)),
            dma((steps,)),
            dma((steps + 1,)),
            dma((steps + 1,)),
            dma(()),
            dma((n_pair,)),
            dma(()),
            dma(()),
            dma(()),
            dma(()),
            pltpu.SemaphoreType.REGULAR((2 + 3,)),
        ],
        compiler_params=pltpu.CompilerParams(
            collective_id=0, has_side_effects=True, vmem_limit_bytes=60 * 1024 * 1024
        ),
        cost_estimate=pl.CostEstimate(
            flops=4 * 10**9, bytes_accessed=5 * 10**6, transcendentals=0
        ),
    )(
        cycle_owner.reshape(1, tiles),
        cycle_slot.reshape(1, tiles),
        ladder_rows[0],
        ladder_count,
        amps,
        pair_energy.reshape(1, slab),
        virt_energy.reshape(1, KP * TB),
        ladder_tiles[0],
        cycle_tiles[0],
    )


def solution(mesh):
    in_specs = (
        P("pair", "panel"),
        P("pair"),
        P("panel"),
        P("pair", "panel", None),
        P("pair", "panel"),
        P("pair", "panel", None, None),
        P(("pair", "panel"), None),
        P(("pair", "panel"), None),
        P("pair", "panel", None, None),
    )
    return jax.shard_map(
        functools.partial(on_device, mesh.shape["pair"], mesh.shape["panel"]),
        mesh=mesh,
        in_specs=in_specs,
        out_specs=P("pair", "panel"),
        check_vma=False,
    )
```
